32 devices in a mesh: ctx: 8 (over z, x), ch: 2 (over y), section: 2 (over core).
Axes of the slice: x: 2, y: 2, z: 4, core: 2. Of those that a mesh axis runs over, the one named last changes fastest.
Arguments:
- mamba_x: bfloat16 [1024, 8192], P('ctx', ('ch', 'section')), may hold values from -6 to 6
- mamba_b: bfloat16 [1024, 1024], P('ctx', ('ch', 'section')), may hold values from -6 to 6
- mamba_c: bfloat16 [1024, 1024], P('ctx', ('ch', 'section')), may hold values from -6 to 6
- step_dt: float32 [1024, 64], P('ctx', ('ch', 'section')), may hold values from 0 to 0.35, as said below
- decay_a: float32 [64], P(('ch', 'section')), may hold values from 0.5 to 2
- skip_d: float32 [64], P(('ch', 'section')), may hold values from 0.5 to 1.5
- value_weight: bfloat16 [8192, 1024], P(('ch', 'section')), may hold values from -0.0625 to 0.0625
- queries: bfloat16 [1024, 8192], P('ctx', ('ch', 'section')), may hold values from -20 to 20
- keys: bfloat16 [1024, 1024], P('ctx', ('ch', 'section')), may hold values from -6 to 6
- out_grad: bfloat16 [1024, 8192], P('ctx', ('ch', 'section')), may hold values from -6 to 6
Outputs:
- attn_out: float32 [1024, 8192], P('ctx', ('ch', 'section'))
- grad_q: float32 [1024, 8192], P('ctx', ('ch', 'section'))
- grad_k: float32 [1024, 1024], P('ctx', ('ch', 'section'))
- grad_x: float32 [1024, 8192], P('ctx', ('ch', 'section'))
- grad_b: float32 [1024, 1024], P('ctx', ('ch', 'section'))
- grad_c: float32 [1024, 1024], P('ctx', ('ch', 'section'))
The draws below stay inside these ranges and needn't reach their ends.
Inputs may be any that keep to these rules, and one draw needn't show every extreme that they name: `step_dt`: positive step sizes.
All inputs are finite; a program needn't handle non-finite values.
Results may differ from the reference program's by a relative error of at most 0.0059.
Values may be sent and summed in bfloat16 or wider, within the bound.
A program may use at most 128 MiB of HBM per device.

```python
import math
import jax
import jax.numpy as jnp
from jax import lax

TOK_DEV = 128
SSM_HEADS = 64
HEAD_P = 128
STATE = 128
GROUPS = 8
Q_HEADS = 64
KV_HEADS = 8
HEAD_DIM = 128
CONTEXT_LENGTH = 1024


def key_field(key):
    base_key = jax.random.fold_in(key, 21)
    field = jax.random.truncated_normal(base_key, -6.0, 6.0, (CONTEXT_LENGTH, KV_HEADS, HEAD_DIM), jnp.float32)
    return field


def draw_keys(key, part):
    field = key_field(key)
    return field.reshape(CONTEXT_LENGTH, KV_HEADS * HEAD_DIM).astype(jnp.bfloat16)


def draw_queries(key, part):
    base_key = jax.random.fold_in(key, 22)
    field = jax.random.truncated_normal(base_key, -6.0, 6.0, (CONTEXT_LENGTH, Q_HEADS, HEAD_DIM), jnp.float32)
    return field.reshape(CONTEXT_LENGTH, Q_HEADS * HEAD_DIM).astype(jnp.bfloat16)


def draw_step_dt(key, part):
    sub_keys = jax.random.split(key, 3)
    fast_share = 0.5
    fast_heads = jax.random.uniform(sub_keys[0], (SSM_HEADS,), jnp.float32) < fast_share
    stochastic_jitter = jnp.exp(jax.random.uniform(sub_keys[1], (CONTEXT_LENGTH, SSM_HEADS), jnp.float32, -math.log(2.0), math.log(2.0)))
    nominal_frequency = jnp.where(fast_heads, 1.0 / 40.0, 0.5 / CONTEXT_LENGTH)
    flagged_locations = jax.random.randint(sub_keys[2], (4,), 0, CONTEXT_LENGTH)
    clustered_arrivals = jnp.any(jnp.arange(CONTEXT_LENGTH)[:, None] == flagged_locations[None, :], axis=1)
    return nominal_frequency[None, :] * stochastic_jitter + jnp.where(clustered_arrivals, 0.3, 0.0)[:, None]


def block_scale(own_key, extent, cuts, least, largest):
    def one(dim, blocks):
        heights = jax.random.uniform(jax.random.fold_in(jax.random.fold_in(own_key, 6), dim), (blocks,), jnp.float32, least / len(cuts), largest / len(cuts))
        return jnp.repeat(jnp.exp(heights), extent[dim] // blocks).reshape((-1,) + (1,) * (len(extent) - dim - 1))

    factor_of = one(*cuts[0])
    for cut in cuts[1:]:
        factor_of = factor_of * one(*cut)
    return factor_of


def scatter_about(rng, extent, width, limit, cuts=(), kind=jnp.bfloat16):
    result = jax.random.normal(rng, extent, jnp.float32) * width
    if len(cuts) > 0:
        result = block_scale(rng, extent, cuts, -0.22, 0.18) * result
    return jnp.clip(result, min=-limit, max=limit).astype(kind)


def setup_inputs(seed: int = 0) -> dict:
    arg_keys = jax.random.split(jax.random.key(seed), 11)
    mamba_x = scatter_about(arg_keys[0], (CONTEXT_LENGTH, SSM_HEADS * HEAD_P), 1.0, 6.0, ((0, 8), (1, 4)))
    mamba_b = scatter_about(arg_keys[1], (CONTEXT_LENGTH, GROUPS * STATE), 1.0, 6.0, ((0, 8), (1, 4)))
    mamba_c = scatter_about(arg_keys[2], (CONTEXT_LENGTH, GROUPS * STATE), 1.0, 6.0, ((0, 8), (1, 4)))
    step_dt = draw_step_dt(jax.random.fold_in(arg_keys[10], 71), 0)
    decay_a = jnp.clip(jnp.exp(math.log(2.0) - 1.3862944 * jax.random.uniform(arg_keys[4], (SSM_HEADS,), jnp.float32) ** block_scale(arg_keys[4], (SSM_HEADS,), ((0, 4),), -0.2, 0.2)), 0.5, 2.0)
    skip_d = jnp.clip(0.5 + 1.0 * jax.random.uniform(arg_keys[5], (SSM_HEADS,), jnp.float32) ** block_scale(arg_keys[5], (SSM_HEADS,), ((0, 4),), -0.2, 0.2), 0.5, 1.5)
    value_weight = scatter_about(arg_keys[6], (SSM_HEADS * HEAD_P, KV_HEADS * HEAD_DIM), (SSM_HEADS * HEAD_P) ** -0.5, 0.0625, ((0, 4),))
    queries = draw_queries(jax.random.fold_in(arg_keys[10], 71), 0)
    keys = draw_keys(jax.random.fold_in(arg_keys[10], 71), 0)
    out_grad = scatter_about(arg_keys[9], (CONTEXT_LENGTH, Q_HEADS * HEAD_DIM), 1.0, 6.0, ((0, 8), (1, 4)))
    return dict(mamba_x=mamba_x, mamba_b=mamba_b, mamba_c=mamba_c, step_dt=step_dt, decay_a=decay_a, skip_d=skip_d, value_weight=value_weight, queries=queries, keys=keys, out_grad=out_grad)


HIGHEST = lax.Precision.HIGHEST
NEG_FILL = -1e+30

def block_terms(inputs_x, inputs_b, inputs_c, step_sizes, decay_rates, skip_gains):
    head_count = inputs_x.shape[1]
    repeat_by = head_count // inputs_b.shape[1]
    log_sums = jnp.cumsum(-step_sizes * decay_rates[None, :], axis=0)
    positions = jnp.arange(log_sums.shape[0])
    lower_mask = (positions[:, None] >= positions[None, :])[None]
    log_gaps = log_sums.T[:, :, None] - log_sums.T[:, None, :]
    decays = jnp.where(lower_mask, jnp.exp(jnp.where(lower_mask, log_gaps, 0.0)), 0.0)
    inner_prod = jnp.einsum('tgn,sgn->gts', inputs_c, inputs_b, precision=HIGHEST)
    inner_prod = jnp.repeat(inner_prod, repeat_by, axis=0)
    mixing = inner_prod * decays * step_sizes.T[:, None, :]
    local_out = jnp.einsum('hts,shp->thp', mixing, inputs_x, precision=HIGHEST) + skip_gains[None, :, None] * inputs_x
    to_end = jnp.exp(log_sums[-1][None, :] - log_sums) * step_sizes
    b_heads = jnp.repeat(inputs_b, repeat_by, axis=1)
    weighted = inputs_x * to_end[:, :, None]
    end_state = jnp.einsum('shp,shn->hpn', weighted, b_heads, precision=HIGHEST)
    return (local_out, end_state, jnp.exp(log_sums[-1]))

def entry_terms(inputs_c, step_sizes, decay_rates, entering):
    repeat_by = entering.shape[0] // inputs_c.shape[1]
    log_sums = jnp.cumsum(-step_sizes * decay_rates[None, :], axis=0)
    c_heads = jnp.repeat(inputs_c, repeat_by, axis=1)
    carried = jnp.einsum('thn,hpn->thp', c_heads, entering, precision=HIGHEST)
    return jnp.exp(log_sums)[:, :, None] * carried

def mamba_forward(x_float, b_float, readout_matrix_single, step_dt, decay_a, skip_d):
    block_count = x_float.shape[0] // TOK_DEV
    x_blocks = x_float.reshape(block_count, TOK_DEV, SSM_HEADS, HEAD_P)
    b_blocks = b_float.reshape(block_count, TOK_DEV, GROUPS, STATE)
    c_blocks = readout_matrix_single.reshape(block_count, TOK_DEV, GROUPS, STATE)
    dt_blocks = step_dt.reshape(block_count, TOK_DEV, SSM_HEADS)
    local_out, end_states, end_decays = jax.vmap(block_terms, in_axes=(0, 0, 0, 0, None, None))(x_blocks, b_blocks, c_blocks, dt_blocks, decay_a, skip_d)

    def advance(running, item_pair):
        return (item_pair[0][:, None, None] * running + item_pair[1], running)
    initial = jnp.zeros((SSM_HEADS, HEAD_P, STATE), jnp.float32)
    _, entering = lax.scan(advance, initial, (end_decays, end_states))
    entry_out = jax.vmap(entry_terms, in_axes=(0, 0, None, 0))(c_blocks, dt_blocks, decay_a, entering)
    return (local_out + entry_out).reshape(x_float.shape[0], SSM_HEADS * HEAD_P)

def attend_group(group_q, group_k, group_v, group_d):
    scale_by = 1.0 / math.sqrt(HEAD_DIM)
    positions = jnp.arange(group_q.shape[0])
    visible = (positions[None, :] <= positions[:, None])[None]
    scores = jnp.einsum('trd,sd->rts', group_q, group_k) * scale_by
    scores = jnp.where(visible, scores, NEG_FILL)
    row_top = lax.optimization_barrier(jnp.max(scores, axis=-1))
    probs = jnp.where(visible, jnp.exp(scores - row_top[..., None]), 0.0)
    probs = probs / lax.optimization_barrier(jnp.sum(probs, axis=-1))[..., None]
    probability_batch = probs.astype(jnp.bfloat16).astype(jnp.float32)
    output = jnp.einsum('rts,sd->trd', probability_batch, group_v)
    dprobs = jnp.einsum('trd,sd->rts', group_d, group_v)
    delta = lax.optimization_barrier(jnp.sum(group_d * output, axis=-1)).T
    dscores = probs * (dprobs - delta[..., None])
    score_gradient_batch = dscores.astype(jnp.bfloat16).astype(jnp.float32)
    query_grad = jnp.einsum('rts,sd->trd', score_gradient_batch, group_k) * scale_by
    key_grad = jnp.einsum('rts,trd->sd', score_gradient_batch, group_q) * scale_by
    value_grad = jnp.einsum('rts,trd->sd', probability_batch, group_d).astype(jnp.bfloat16)
    return (output, query_grad, key_grad, value_grad)

def reference(mamba_x, mamba_b, mamba_c, step_dt, decay_a, skip_d, value_weight, queries, keys, out_grad):
    x_float = mamba_x.astype(jnp.float32)
    b_float = mamba_b.astype(jnp.float32)
    readout_matrix_single = mamba_c.astype(jnp.float32)

    def forward(arg_x, arg_b, arg_c):
        return mamba_forward(arg_x, arg_b, arg_c, step_dt, decay_a, skip_d)
    mamba_y, pullback = jax.vjp(forward, x_float, b_float, readout_matrix_single)
    values = jnp.dot(mamba_y.astype(jnp.bfloat16), value_weight, preferred_element_type=jnp.float32).astype(jnp.bfloat16)
    rep_count = Q_HEADS // KV_HEADS
    grouped_q = queries.astype(jnp.float32).reshape(CONTEXT_LENGTH, KV_HEADS, rep_count, HEAD_DIM).transpose(1, 0, 2, 3)
    grouped_d = out_grad.astype(jnp.float32).reshape(CONTEXT_LENGTH, KV_HEADS, rep_count, HEAD_DIM).transpose(1, 0, 2, 3)
    grouped_k = keys.astype(jnp.float32).reshape(CONTEXT_LENGTH, KV_HEADS, HEAD_DIM).transpose(1, 0, 2)
    grouped_v = values.astype(jnp.float32).reshape(CONTEXT_LENGTH, KV_HEADS, HEAD_DIM).transpose(1, 0, 2)
    outputs, query_grads, key_grads, value_grads = lax.map(lambda packed: attend_group(packed[0], packed[1], packed[2], packed[3]), (grouped_q, grouped_k, grouped_v, grouped_d))
    attn_out = outputs.transpose(1, 0, 2, 3).reshape(CONTEXT_LENGTH, Q_HEADS * HEAD_DIM)
    grad_q = query_grads.transpose(1, 0, 2, 3).reshape(CONTEXT_LENGTH, Q_HEADS * HEAD_DIM)
    grad_k = key_grads.transpose(1, 0, 2).reshape(CONTEXT_LENGTH, KV_HEADS * HEAD_DIM)
    value_grad = value_grads.transpose(1, 0, 2).reshape(CONTEXT_LENGTH, KV_HEADS * HEAD_DIM)
    mamba_grad = jnp.dot(value_grad, value_weight.T, preferred_element_type=jnp.float32)
    grad_x, grad_b, grad_c = pullback(mamba_grad)
    return (attn_out, grad_q, grad_k, grad_x, grad_b, grad_c)
```

```python
import functools
import math

import jax
import jax.numpy as jnp
from jax import lax
from jax.experimental import pallas as pl
from jax.experimental.pallas import tpu as pltpu
from jax.sharding import PartitionSpec as P

LANE = 128
Q_HEADS = 64
KV_HEADS = 8
REP = Q_HEADS // KV_HEADS
NEG_FILL = -1e30
F32 = jnp.float32
BF16 = jnp.bfloat16
MESH = pl.DeviceIdType.MESH
VMEM_BYTES = 56 * 1024 * 1024


def nn(a, b):
    return lax.dot_general(a, b, (((1,), (0,)), ((), ())), preferred_element_type=F32)


def nt(a, b):
    return lax.dot_general(a, b, (((1,), (1,)), ((), ())), preferred_element_type=F32)


def flip(a):
    return a.astype(F32).T.astype(BF16)


def rounded(a):
    return a.astype(BF16)


def ctx_peer(me, hop, count):
    return lax.rem(me + hop, count)


def group_place(sizes):
    return lax.axis_index("ch") * sizes[1] + lax.axis_index("section")


def group_id(place, sizes):
    return {"ch": place // sizes[1], "section": lax.rem(place, sizes[1])}


def enter(ctx_count, sizes):
    me = lax.axis_index("ctx")
    mine = group_place(sizes)
    members = sizes[0] * sizes[1]
    barrier = pltpu.get_barrier_semaphore()
    for hop in range(1, ctx_count):
        pl.semaphore_signal(
            barrier, inc=1, device_id={"ctx": ctx_peer(me, hop, ctx_count)}, device_id_type=MESH
        )
    for hop in range(1, members):
        pl.semaphore_signal(
            barrier,
            inc=1,
            device_id=group_id(lax.rem(mine + hop, members), sizes),
            device_id_type=MESH,
        )
    pl.semaphore_wait(barrier, ctx_count + members - 2)


def enter_ctx(ctx_count):
    me = lax.axis_index("ctx")
    barrier = pltpu.get_barrier_semaphore()
    for hop in range(1, ctx_count):
        pl.semaphore_signal(
            barrier, inc=1, device_id={"ctx": ctx_peer(me, hop, ctx_count)}, device_id_type=MESH
        )
    pl.semaphore_wait(barrier, ctx_count - 1)


def remote(src, dst, send, recv, device):
    return pltpu.make_async_remote_copy(
        src_ref=src, dst_ref=dst, send_sem=send, recv_sem=recv, device_id=device, device_id_type=MESH
    )


def triangle(rows, lower):
    first = lax.broadcasted_iota(jnp.int32, (rows, rows), 0)
    second = lax.broadcasted_iota(jnp.int32, (rows, rows), 1)
    return first >= second if lower else second >= first


def scan_parts(me, rows):
    width = min(rows, LANE)
    for part in range(rows // width):
        yield slice(part * width, (part + 1) * width), (me * rows + part * width) // LANE


def forward_kernel(
    ctx_count, sizes,
    x_ref, b_ref, c_ref, cum_ref, cumt_ref, dt_ref, dtt_ref, skip_ref, dec_ref, w_ref, k_ref,
    kall_out, vall_out, ent_out, decall_out,
    kall, vall, decall, st_send, st_recv, en_send, en_recv, y_acc, y_b, vp_send, vp_recv,
    st_s, st_r, en_s, en_r, k_s, k_r, v_s, v_r, d_s, d_r, p_s, p_r,
):
    me = lax.axis_index("ctx")
    mine = group_place(sizes)
    members = sizes[0] * sizes[1]
    tok = x_ref.shape[0]
    heads = x_ref.shape[1] // LANE
    per_group = heads // (b_ref.shape[1] // LANE)
    rows = heads * LANE // ctx_count
    kall[...] = jnp.zeros_like(kall)
    vall[...] = jnp.zeros_like(vall)
    enter(ctx_count, sizes)
    decall[me] = dec_ref[...]
    kall[me] = k_ref[...]
    for head in range(heads):
        group = head // per_group
        if head % per_group == 0:
            b_flip = flip(b_ref[:, group * LANE:(group + 1) * LANE])
        cum = cum_ref[:, head:head + 1]
        weight = jnp.exp(cum[tok - 1:tok, :] - cum) * dt_ref[:, head:head + 1]
        xw = x_ref[:, head * LANE:(head + 1) * LANE].astype(F32) * weight
        st_send[head * LANE:(head + 1) * LANE, :] = rounded(nn(b_flip, rounded(xw)))
    sends = []
    for hop in range(1, ctx_count):
        peer = ctx_peer(me, hop, ctx_count)
        to = {"ctx": peer}
        copy = remote(decall.at[me], decall.at[me], d_s.at[hop], d_r.at[hop], to)
        copy.start()
        sends.append(copy)
        block = pl.ds(pl.multiple_of(peer * rows, 16), rows)
        copy = remote(st_send.at[block], st_recv.at[me], st_s.at[hop], st_r.at[hop], to)
        copy.start()
        sends.append(copy)
    for hop in range(1, ctx_count):
        peer = ctx_peer(me, hop, ctx_count)

        @pl.when(peer > me)
        def _():
            remote(kall.at[me], kall.at[me], k_s.at[hop], k_r.at[hop], {"ctx": peer}).start()

    st_recv[me] = st_send[pl.ds(pl.multiple_of(me * rows, 16), rows), :]
    lower = triangle(tok, True)
    for head in range(heads):
        group = head // per_group
        if head % per_group == 0:
            columns = slice(group * LANE, (group + 1) * LANE)
            inner = nt(c_ref[:, columns], b_ref[:, columns])
        gap = cum_ref[:, head:head + 1] - cumt_ref[head:head + 1, :]
        decays = jnp.where(lower, jnp.exp(jnp.where(lower, gap, 0.0)), 0.0)
        mixing = inner * decays * dtt_ref[head:head + 1, :]
        high = rounded(mixing)
        low = rounded(mixing - high.astype(F32))
        x_head = x_ref[:, head * LANE:(head + 1) * LANE]
        y_acc[:, head * LANE:(head + 1) * LANE] = (
            nn(high, x_head) + nn(low, x_head) + skip_ref[:, head:head + 1] * x_head.astype(F32)
        )
    for hop in range(1, ctx_count):
        peer = ctx_peer(me, ctx_count - hop, ctx_count)
        to = {"ctx": peer}
        remote(decall.at[me], decall.at[peer], d_s.at[hop], d_r.at[hop], to).wait_recv()
        remote(
            st_send.at[pl.ds(0, rows)], st_recv.at[peer], st_s.at[hop], st_r.at[hop], to
        ).wait_recv()
    running = [jnp.zeros((part.stop - part.start, LANE), F32) for part, _ in scan_parts(me, rows)]
    for block in range(ctx_count):
        for at, (part, head) in enumerate(scan_parts(me, rows)):
            en_send[block, part, :] = rounded(running[at])
            running[at] = (
                decall[block, pl.ds(head, 1), :] * running[at] + st_recv[block, part, :].astype(F32)
            )
    own_rows = pl.ds(pl.multiple_of(me * rows, 16), rows)
    for hop in range(1, ctx_count):
        peer = ctx_peer(me, hop, ctx_count)
        copy = remote(
            en_send.at[peer], en_recv.at[own_rows], en_s.at[hop], en_r.at[hop], {"ctx": peer}
        )
        copy.start()
        sends.append(copy)
    en_recv[own_rows, :] = en_send[me]
    for hop in range(1, ctx_count):
        peer = ctx_peer(me, ctx_count - hop, ctx_count)
        block = pl.ds(pl.multiple_of(peer * rows, 16), rows)
        remote(
            en_send.at[0], en_recv.at[block], en_s.at[hop], en_r.at[hop], {"ctx": peer}
        ).wait_recv()
    for head in range(heads):
        group = head // per_group
        span = slice(head * LANE, (head + 1) * LANE)
        carried = nn(c_ref[:, group * LANE:(group + 1) * LANE], en_recv[span, :])
        y_b[:, span] = rounded(y_acc[:, span] + jnp.exp(cum_ref[:, head:head + 1]) * carried)
    kv = k_ref.shape[1]
    for hop in list(range(1, members)) + [0]:
        place = lax.rem(mine + hop, members)
        piece = nn(y_b[...], w_ref[:, pl.ds(pl.multiple_of(place * kv, LANE), kv)])
        if hop:
            vp_send[hop] = rounded(piece)
            copy = remote(
                vp_send.at[hop], vp_recv.at[hop], p_s.at[hop], p_r.at[hop], group_id(place, sizes)
            )
            copy.start()
            sends.append(copy)
    for hop in range(1, members):
        place = lax.rem(mine + hop, members)
        remote(
            vp_send.at[hop], vp_recv.at[hop], p_s.at[hop], p_r.at[hop], group_id(place, sizes)
        ).wait_recv()
        piece = piece + vp_recv[hop].astype(F32)
    vall[me] = rounded(piece)
    for hop in range(1, ctx_count):
        peer = ctx_peer(me, hop, ctx_count)

        @pl.when(peer > me)
        def _():
            remote(vall.at[me], vall.at[me], v_s.at[hop], v_r.at[hop], {"ctx": peer}).start()

    for hop in range(1, ctx_count):
        source = ctx_peer(me, ctx_count - hop, ctx_count)

        @pl.when(source < me)
        def _():
            to = {"ctx": source}
            remote(kall.at[me], kall.at[source], k_s.at[hop], k_r.at[hop], to).wait_recv()
            remote(vall.at[me], vall.at[source], v_s.at[hop], v_r.at[hop], to).wait_recv()

    kall_out[...] = kall[...]
    vall_out[...] = vall[...]
    ent_out[...] = en_recv[...]
    decall_out[...] = decall[...]
    for copy in sends:
        copy.wait_send()
    for hop in range(1, ctx_count):
        peer = ctx_peer(me, hop, ctx_count)

        @pl.when(peer > me)
        def _():
            to = {"ctx": peer}
            remote(kall.at[me], kall.at[me], k_s.at[hop], k_r.at[hop], to).wait_send()
            remote(vall.at[me], vall.at[me], v_s.at[hop], v_r.at[hop], to).wait_send()


def attention_kernel(
    ctx_count, sizes,
    q_ref, do_ref, kall_ref, vall_ref,
    o_ref, dq_ref, dk_ref, vg_out,
    k_flip, v_flip, s_buf, dp_buf, dk_acc, dv_acc, g_send, g_recv, vg_all,
    g_s, g_r, vg_s, vg_r,
):
    me = lax.axis_index("ctx")
    mine = group_place(sizes)
    members = sizes[0] * sizes[1]
    tok = q_ref.shape[0]
    seq = kall_ref.shape[0]
    kv_dev = kall_ref.shape[1] // LANE
    chunk = math.gcd(seq, 256)
    chunks = (me * tok + tok - 1) // chunk + 1
    scale_by = 1.0 / math.sqrt(LANE)
    pair = 2 * LANE
    cols = 2 * tok
    g_recv[...] = jnp.zeros_like(g_recv)
    dk_acc[...] = jnp.zeros_like(dk_acc)
    dv_acc[...] = jnp.zeros_like(dv_acc)
    enter(ctx_count, sizes)
    query_pos = me * tok + lax.rem(lax.broadcasted_iota(jnp.int32, (chunk, cols), 1), tok)
    key_pos = lax.broadcasted_iota(jnp.int32, (chunk, cols), 0)

    for kv in range(kv_dev):
        span = slice(kv * LANE, (kv + 1) * LANE)

        def flip_chunk(at, carry):
            here = pl.ds(pl.multiple_of(at * chunk, LANE), chunk)
            k_flip[:, here] = flip(kall_ref[here, span])
            v_flip[:, here] = flip(vall_ref[here, span])
            return carry

        lax.fori_loop(0, chunks, flip_chunk, 0)

        def one_pair(index, carry):
            first = pl.multiple_of(kv * REP * LANE + index * pair, pair)
            second = pl.multiple_of(first + LANE, LANE)
            q = jnp.concatenate([q_ref[:, pl.ds(first, LANE)], q_ref[:, pl.ds(second, LANE)]], axis=0)
            do = jnp.concatenate(
                [do_ref[:, pl.ds(first, LANE)], do_ref[:, pl.ds(second, LANE)]], axis=0
            )
            q_t = flip(q)
            do_f = do.astype(F32).T
            do_t = do_f.astype(BF16)

            def scores(at, top):
                here = pl.ds(pl.multiple_of(at * chunk, LANE), chunk)
                s = nn(kall_ref[here, span], q_t) * scale_by
                s = jnp.where(key_pos + at * chunk <= query_pos, s, NEG_FILL)
                s_buf[here, :] = s
                return jnp.maximum(top, jnp.max(s, axis=0, keepdims=True))

            top = lax.fori_loop(0, chunks, scores, jnp.full((1, cols), NEG_FILL, F32))

            def totals(at, total):
                here = pl.ds(pl.multiple_of(at * chunk, LANE), chunk)
                e = jnp.exp(s_buf[here, :] - top)
                s_buf[here, :] = e
                dp_buf[here, :] = nn(vall_ref[here, span], do_t)
                return total + jnp.sum(e, axis=0, keepdims=True)

            total = lax.fori_loop(0, chunks, totals, jnp.zeros((1, cols), F32))
            inverse = 1.0 / total

            def outputs(at, o_t):
                here = pl.ds(pl.multiple_of(at * chunk, LANE), chunk)
                p = s_buf[here, :] * inverse
                s_buf[here, :] = p
                p_b = rounded(p)
                dv_acc[here, span] += nn(p_b, do)
                return o_t + nn(v_flip[:, here], p_b)

            o_t = lax.fori_loop(0, chunks, outputs, jnp.zeros((LANE, cols), F32))
            delta = jnp.sum(o_t * do_f, axis=0, keepdims=True)

            def grads(at, dq_t):
                here = pl.ds(pl.multiple_of(at * chunk, LANE), chunk)
                ds = rounded(s_buf[here, :] * (dp_buf[here, :] - delta))
                dk_acc[here, span] += nn(ds, q)
                return dq_t + nn(k_flip[:, here], ds)

            dq_t = lax.fori_loop(0, chunks, grads, jnp.zeros((LANE, cols), F32)) * scale_by
            o_ref[:, pl.ds(first, LANE)] = o_t[:, :tok].T
            o_ref[:, pl.ds(second, LANE)] = o_t[:, tok:].T
            dq_ref[:, pl.ds(first, LANE)] = dq_t[:, :tok].T
            dq_ref[:, pl.ds(second, LANE)] = dq_t[:, tok:].T
            return carry

        lax.fori_loop(0, REP // 2, one_pair, 0)
        for hop in range(1, ctx_count):
            peer = ctx_peer(me, hop, ctx_count)

            @pl.when(peer < me)
            def _():
                block = pl.ds(pl.multiple_of(peer * tok, tok), tok)
                g_send[kv, hop, 0] = rounded(dk_acc[block, span])
                g_send[kv, hop, 1] = rounded(dv_acc[block, span])
                remote(
                    g_send.at[kv, hop], g_recv.at[kv, hop], g_s.at[kv, hop], g_r.at[kv, hop],
                    {"ctx": peer},
                ).start()

    own = pl.ds(pl.multiple_of(me * tok, tok), tok)
    for kv in range(kv_dev):
        span = slice(kv * LANE, (kv + 1) * LANE)
        dk = dk_acc[own, span]
        dv = dv_acc[own, span]
        for hop in range(1, ctx_count):
            source = ctx_peer(me, ctx_count - hop, ctx_count)

            @pl.when(source > me)
            def _():
                remote(
                    g_send.at[kv, hop], g_recv.at[kv, hop], g_s.at[kv, hop], g_r.at[kv, hop],
                    {"ctx": source},
                ).wait_recv()

            dk = dk + g_recv[kv, hop, 0].astype(F32)
            dv = dv + g_recv[kv, hop, 1].astype(F32)
        dk_ref[:, span] = dk * scale_by
        vg_all[mine, :, span] = rounded(dv)
    sends = []
    for hop in range(1, members):
        place = lax.rem(mine + hop, members)
        copy = remote(
            vg_all.at[mine], vg_all.at[mine], vg_s.at[hop], vg_r.at[hop], group_id(place, sizes)
        )
        copy.start()
        sends.append(copy)
    for hop in range(1, members):
        place = lax.rem(mine + members - hop, members)
        remote(
            vg_all.at[mine], vg_all.at[place], vg_s.at[hop], vg_r.at[hop], group_id(place, sizes)
        ).wait_recv()
    vg_out[...] = vg_all[...]
    for copy in sends:
        copy.wait_send()
    for kv in range(kv_dev):
        for hop in range(1, ctx_count):
            peer = ctx_peer(me, hop, ctx_count)

            @pl.when(peer < me)
            def _():
                remote(
                    g_send.at[kv, hop], g_recv.at[kv, hop], g_s.at[kv, hop], g_r.at[kv, hop],
                    {"ctx": peer},
                ).wait_send()


def backward_kernel(
    ctx_count,
    x_ref, b_ref, c_ref, cum_ref, cumt_ref, dt_ref, dtt_ref, skip_ref, w_ref, ent_ref, decall, vg_ref,
    dx_ref, db_ref, dc_ref,
    g_acc, st_send, st_recv, en_send, en_recv,
    st_s, st_r, en_s, en_r,
):
    me = lax.axis_index("ctx")
    tok = x_ref.shape[0]
    heads = x_ref.shape[1] // LANE
    groups = b_ref.shape[1] // LANE
    per_group = heads // groups
    rows = heads * LANE // ctx_count
    kv = vg_ref.shape[2]
    enter_ctx(ctx_count)
    for group in range(groups):
        wide = slice(group * per_group * LANE, (group + 1) * per_group * LANE)
        total = None
        for place in range(vg_ref.shape[0]):
            term = nt(vg_ref[place], w_ref[wide, place * kv:(place + 1) * kv])
            total = term if total is None else total + term
        g_acc[:, wide] = total
        c_flip = flip(c_ref[:, group * LANE:(group + 1) * LANE])
        for head in range(group * per_group, (group + 1) * per_group):
            span = slice(head * LANE, (head + 1) * LANE)
            scaled = rounded(jnp.exp(cum_ref[:, head:head + 1]) * g_acc[:, span])
            st_send[span, :] = rounded(nn(c_flip, scaled))
    sends = []
    for hop in range(1, ctx_count):
        peer = ctx_peer(me, hop, ctx_count)
        block = pl.ds(pl.multiple_of(peer * rows, 16), rows)
        copy = remote(st_send.at[block], st_recv.at[me], st_s.at[hop], st_r.at[hop], {"ctx": peer})
        copy.start()
        sends.append(copy)
    own_rows = pl.ds(pl.multiple_of(me * rows, 16), rows)
    st_recv[me] = st_send[own_rows, :]
    lower = triangle(tok, True)
    upper = triangle(tok, False)
    for group in range(groups):
        columns = slice(group * LANE, (group + 1) * LANE)
        b = b_ref[:, columns]
        c = c_ref[:, columns]
        inner_t = nt(b, c)
        inner_grad = jnp.zeros((tok, tok), F32)
        dc = jnp.zeros((tok, LANE), F32)
        for head in range(group * per_group, (group + 1) * per_group):
            span = slice(head * LANE, (head + 1) * LANE)
            cum = cum_ref[:, head:head + 1]
            cum_t = cumt_ref[head:head + 1, :]
            decays = jnp.where(lower, jnp.exp(jnp.where(lower, cum - cum_t, 0.0)), 0.0)
            decays_t = jnp.where(upper, jnp.exp(jnp.where(upper, cum_t - cum, 0.0)), 0.0)
            mixing_t = rounded(inner_t * decays_t * dt_ref[:, head:head + 1])
            g = g_acc[:, span]
            g_b = rounded(g)
            dx_ref[:, span] = nn(mixing_t, g_b) + skip_ref[:, head:head + 1] * g
            inner_grad = inner_grad + nt(g_b, x_ref[:, span]) * decays * dtt_ref[head:head + 1, :]
            dc = dc + nt(rounded(jnp.exp(cum) * g), ent_ref[span, :])
        dc_ref[:, columns] = dc + nn(rounded(inner_grad), b)
        db_ref[:, columns] = nn(rounded(inner_grad.T), c)
    for hop in range(1, ctx_count):
        peer = ctx_peer(me, ctx_count - hop, ctx_count)
        remote(
            st_send.at[pl.ds(0, rows)], st_recv.at[peer], st_s.at[hop], st_r.at[hop], {"ctx": peer}
        ).wait_recv()
    running = [jnp.zeros((part.stop - part.start, LANE), F32) for part, _ in scan_parts(me, rows)]
    for block in range(ctx_count - 1, -1, -1):
        for at, (part, head) in enumerate(scan_parts(me, rows)):
            en_send[block, part, :] = rounded(running[at])
            running[at] = (
                decall[block, pl.ds(head, 1), :] * running[at] + st_recv[block, part, :].astype(F32)
            )
    for hop in range(1, ctx_count):
        peer = ctx_peer(me, hop, ctx_count)
        copy = remote(
            en_send.at[peer], en_recv.at[own_rows], en_s.at[hop], en_r.at[hop], {"ctx": peer}
        )
        copy.start()
        sends.append(copy)
    en_recv[own_rows, :] = en_send[me]
    for hop in range(1, ctx_count):
        peer = ctx_peer(me, ctx_count - hop, ctx_count)
        block = pl.ds(pl.multiple_of(peer * rows, 16), rows)
        remote(
            en_send.at[0], en_recv.at[block], en_s.at[hop], en_r.at[hop], {"ctx": peer}
        ).wait_recv()
    for group in range(groups):
        columns = slice(group * LANE, (group + 1) * LANE)
        b = b_ref[:, columns]
        db = db_ref[:, columns]
        for head in range(group * per_group, (group + 1) * per_group):
            span = slice(head * LANE, (head + 1) * LANE)
            cum = cum_ref[:, head:head + 1]
            weight = jnp.exp(cum[tok - 1:tok, :] - cum) * dt_ref[:, head:head + 1]
            dstate = en_recv[span, :]
            dx_ref[:, span] += weight * nn(b, dstate)
            db = db + nt(rounded(x_ref[:, span].astype(F32) * weight), dstate)
        db_ref[:, columns] = db
    for copy in sends:
        copy.wait_send()


def body(
    sizes,
    mamba_x, mamba_b, mamba_c, step_dt, decay_a, skip_d, value_weight, queries, keys, out_grad
):
    tok = mamba_x.shape[0]
    heads = decay_a.shape[0]
    n = lax.axis_size("ctx")
    members = sizes[0] * sizes[1]
    kv = keys.shape[1]
    kv_dev = kv // LANE
    seq = n * tok
    rows = heads * LANE // n
    cum = jnp.cumsum(-step_dt * decay_a[None, :], axis=0)
    cum_t = cum.T
    dt_t = step_dt.T
    skip = skip_d[None, :]
    decay = jnp.broadcast_to(jnp.exp(cum[-1])[:, None], (heads, LANE))
    vmem = pl.BlockSpec(memory_space=pltpu.VMEM)
    dma = pltpu.SemaphoreType.DMA

    def call(kernel, operands, outs, scratch, ident):
        return pl.pallas_call(
            kernel,
            out_shape=[jax.ShapeDtypeStruct(shape, kind) for shape, kind in outs],
            in_specs=[vmem] * len(operands),
            out_specs=[vmem] * len(outs),
            scratch_shapes=scratch,
            compiler_params=pltpu.CompilerParams(
                collective_id=ident, has_side_effects=True, vmem_limit_bytes=VMEM_BYTES
            ),
        )(*operands)

    kall, vall, ent, decall = call(
        functools.partial(forward_kernel, n, sizes),
        (mamba_x, mamba_b, mamba_c, cum, cum_t, step_dt, dt_t, skip, decay, value_weight, keys),
        [((n, tok, kv), BF16), ((n, tok, kv), BF16), ((heads * LANE, LANE), BF16),
         ((n, heads, LANE), F32)],
        [
            pltpu.VMEM((n, tok, kv), BF16),
            pltpu.VMEM((n, tok, kv), BF16),
            pltpu.VMEM((n, heads, LANE), F32),
            pltpu.VMEM((heads * LANE, LANE), BF16),
            pltpu.VMEM((n, rows, LANE), BF16),
            pltpu.VMEM((n, rows, LANE), BF16),
            pltpu.VMEM((heads * LANE, LANE), BF16),
            pltpu.VMEM((tok, heads * LANE), F32),
            pltpu.VMEM((tok, heads * LANE), BF16),
            pltpu.VMEM((members, tok, kv), BF16),
            pltpu.VMEM((members, tok, kv), BF16),
        ] + [dma((n,))] * 10 + [dma((members,))] * 2,
        0,
    )
    attn_out, grad_q, grad_k, vg = call(
        functools.partial(attention_kernel, n, sizes),
        (queries, out_grad, kall.reshape(seq, kv), vall.reshape(seq, kv)),
        [(queries.shape, F32), (queries.shape, F32), (keys.shape, F32), ((members, tok, kv), BF16)],
        [
            pltpu.VMEM((LANE, seq), BF16),
            pltpu.VMEM((LANE, seq), BF16),
            pltpu.VMEM((seq, 2 * tok), F32),
            pltpu.VMEM((seq, 2 * tok), F32),
            pltpu.VMEM((seq, kv), F32),
            pltpu.VMEM((seq, kv), F32),
            pltpu.VMEM((kv_dev, n, 2, tok, LANE), BF16),
            pltpu.VMEM((kv_dev, n, 2, tok, LANE), BF16),
            pltpu.VMEM((members, tok, kv), BF16),
            dma((kv_dev, n)), dma((kv_dev, n)), dma((members,)), dma((members,)),
        ],
        1,
    )
    grad_x, grad_b, grad_c = call(
        functools.partial(backward_kernel, n),
        (mamba_x, mamba_b, mamba_c, cum, cum_t, step_dt, dt_t, skip, value_weight, ent, decall, vg),
        [(mamba_x.shape, F32), (mamba_b.shape, F32), (mamba_c.shape, F32)],
        [
            pltpu.VMEM((tok, heads * LANE), F32),
            pltpu.VMEM((heads * LANE, LANE), BF16),
            pltpu.VMEM((n, rows, LANE), BF16),
            pltpu.VMEM((n, rows, LANE), BF16),
            pltpu.VMEM((heads * LANE, LANE), BF16),
        ] + [dma((n,))] * 4,
        2,
    )
    return (attn_out, grad_q, grad_k, grad_x, grad_b, grad_c)


def solution(mesh):
    split = P("ctx", ("ch", "section"))
    per_head = P(("ch", "section"))
    in_specs = (
        split, split, split, split, per_head, per_head, P(("ch", "section"), None), split, split, split
    )
    sizes = (mesh.shape["ch"], mesh.shape["section"])
    return jax.shard_map(
        functools.partial(body, sizes),
        mesh=mesh, in_specs=in_specs, out_specs=(split,) * 6, check_vma=False,
    )
```

```python
import functools
import math

import jax
import jax.numpy as jnp
from jax import lax
from jax.experimental import pallas as pl
from jax.experimental.pallas import tpu as pltpu
from jax.sharding import PartitionSpec as P

LANE = 128
Q_HEADS = 64
KV_HEADS = 8
REP = Q_HEADS // KV_HEADS
NEG_FILL = -1e30
F32 = jnp.float32
BF16 = jnp.bfloat16
MESH = pl.DeviceIdType.MESH
VMEM_BYTES = 56 * 1024 * 1024


def nn(a, b):
    return lax.dot_general(a, b, (((1,), (0,)), ((), ())), preferred_element_type=F32)


def nt(a, b):
    return lax.dot_general(a, b, (((1,), (1,)), ((), ())), preferred_element_type=F32)


def flip(a):
    return a.astype(F32).T.astype(BF16)


def rounded(a):
    return a.astype(BF16)


def ctx_peer(me, hop, count):
    return lax.rem(me + hop, count)


def group_place(sizes):
    return lax.axis_index("ch") * sizes[1] + lax.axis_index("section")


def group_id(place, sizes):
    return {"ch": place // sizes[1], "section": lax.rem(place, sizes[1])}


def enter(ctx_count, sizes):
    me = lax.axis_index("ctx")
    mine = group_place(sizes)
    members = sizes[0] * sizes[1]
    barrier = pltpu.get_barrier_semaphore()
    for hop in range(1, ctx_count):
        pl.semaphore_signal(
            barrier, inc=1, device_id={"ctx": ctx_peer(me, hop, ctx_count)}, device_id_type=MESH
        )
    for hop in range(1, members):
        pl.semaphore_signal(
            barrier,
            inc=1,
            device_id=group_id(lax.rem(mine + hop, members), sizes),
            device_id_type=MESH,
        )
    pl.semaphore_wait(barrier, ctx_count + members - 2)


def enter_ctx(ctx_count):
    me = lax.axis_index("ctx")
    barrier = pltpu.get_barrier_semaphore()
    for hop in range(1, ctx_count):
        pl.semaphore_signal(
            barrier, inc=1, device_id={"ctx": ctx_peer(me, hop, ctx_count)}, device_id_type=MESH
        )
    pl.semaphore_wait(barrier, ctx_count - 1)


def remote(src, dst, send, recv, device):
    return pltpu.make_async_remote_copy(
        src_ref=src, dst_ref=dst, send_sem=send, recv_sem=recv, device_id=device, device_id_type=MESH
    )


def triangle(rows, lower):
    first = lax.broadcasted_iota(jnp.int32, (rows, rows), 0)
    second = lax.broadcasted_iota(jnp.int32, (rows, rows), 1)
    return first >= second if lower else second >= first


def scan_parts(me, rows):
    width = min(rows, LANE)
    for part in range(rows // width):
        yield slice(part * width, (part + 1) * width), (me * rows + part * width) // LANE


def forward_kernel(
    ctx_count, sizes,
    x_ref, b_ref, c_ref, cum_ref, cumt_ref, dt_ref, dtt_ref, skip_ref, dec_ref, w_hbm, k_ref,
    kall_out, vall_out, ent_out, decall_out,
    kall, vall, decall, st_send, st_recv, en_send, en_recv, y_acc, y_b, vp_send, vp_recv,
    st_s, st_r, en_s, en_r, k_s, k_r, v_s, v_r, d_s, d_r, p_s, p_r, w_ref, w_s,
):
    me = lax.axis_index("ctx")
    mine = group_place(sizes)
    members = sizes[0] * sizes[1]
    tok = x_ref.shape[0]
    heads = x_ref.shape[1] // LANE
    per_group = heads // (b_ref.shape[1] // LANE)
    rows = heads * LANE // ctx_count
    load = pltpu.make_async_copy(w_hbm, w_ref, w_s)
    load.start()
    kall[...] = jnp.zeros_like(kall)
    vall[...] = jnp.zeros_like(vall)
    enter(ctx_count, sizes)
    decall[me] = dec_ref[...]
    kall[me] = k_ref[...]
    for head in range(heads):
        group = head // per_group
        if head % per_group == 0:
            b_flip = flip(b_ref[:, group * LANE:(group + 1) * LANE])
        cum = cum_ref[:, head:head + 1]
        weight = jnp.exp(cum[tok - 1:tok, :] - cum) * dt_ref[:, head:head + 1]
        xw = x_ref[:, head * LANE:(head + 1) * LANE].astype(F32) * weight
        st_send[head * LANE:(head + 1) * LANE, :] = rounded(nn(b_flip, rounded(xw)))
    sends = []
    for hop in range(1, ctx_count):
        peer = ctx_peer(me, hop, ctx_count)
        to = {"ctx": peer}
        copy = remote(decall.at[me], decall.at[me], d_s.at[hop], d_r.at[hop], to)
        copy.start()
        sends.append(copy)
        block = pl.ds(pl.multiple_of(peer * rows, 16), rows)
        copy = remote(st_send.at[block], st_recv.at[me], st_s.at[hop], st_r.at[hop], to)
        copy.start()
        sends.append(copy)
    for hop in range(1, ctx_count):
        peer = ctx_peer(me, hop, ctx_count)

        @pl.when(peer > me)
        def _():
            remote(kall.at[me], kall.at[me], k_s.at[hop], k_r.at[hop], {"ctx": peer}).start()

    st_recv[me] = st_send[pl.ds(pl.multiple_of(me * rows, 16), rows), :]
    lower = triangle(tok, True)
    for head in range(heads):
        group = head // per_group
        if head % per_group == 0:
            columns = slice(group * LANE, (group + 1) * LANE)
            inner = nt(c_ref[:, columns], b_ref[:, columns])
        gap = cum_ref[:, head:head + 1] - cumt_ref[head:head + 1, :]
        decays = jnp.where(lower, jnp.exp(jnp.where(lower, gap, 0.0)), 0.0)
        mixing = inner * decays * dtt_ref[head:head + 1, :]
        high = rounded(mixing)
        low = rounded(mixing - high.astype(F32))
        x_head = x_ref[:, head * LANE:(head + 1) * LANE]
        y_acc[:, head * LANE:(head + 1) * LANE] = (
            nn(high, x_head) + nn(low, x_head) + skip_ref[:, head:head + 1] * x_head.astype(F32)
        )
    for hop in range(1, ctx_count):
        peer = ctx_peer(me, ctx_count - hop, ctx_count)
        to = {"ctx": peer}
        remote(decall.at[me], decall.at[peer], d_s.at[hop], d_r.at[hop], to).wait_recv()
        remote(
            st_send.at[pl.ds(0, rows)], st_recv.at[peer], st_s.at[hop], st_r.at[hop], to
        ).wait_recv()
    running = [jnp.zeros((part.stop - part.start, LANE), F32) for part, _ in scan_parts(me, rows)]
    for block in range(ctx_count):
        for at, (part, head) in enumerate(scan_parts(me, rows)):
            en_send[block, part, :] = rounded(running[at])
            running[at] = (
                decall[block, pl.ds(head, 1), :] * running[at] + st_recv[block, part, :].astype(F32)
            )
    own_rows = pl.ds(pl.multiple_of(me * rows, 16), rows)
    for hop in range(1, ctx_count):
        peer = ctx_peer(me, hop, ctx_count)
        copy = remote(
            en_send.at[peer], en_recv.at[own_rows], en_s.at[hop], en_r.at[hop], {"ctx": peer}
        )
        copy.start()
        sends.append(copy)
    en_recv[own_rows, :] = en_send[me]
    for hop in range(1, ctx_count):
        peer = ctx_peer(me, ctx_count - hop, ctx_count)
        block = pl.ds(pl.multiple_of(peer * rows, 16), rows)
        remote(
            en_send.at[0], en_recv.at[block], en_s.at[hop], en_r.at[hop], {"ctx": peer}
        ).wait_recv()
    for head in range(heads):
        group = head // per_group
        span = slice(head * LANE, (head + 1) * LANE)
        carried = nn(c_ref[:, group * LANE:(group + 1) * LANE], en_recv[span, :])
        y_b[:, span] = rounded(y_acc[:, span] + jnp.exp(cum_ref[:, head:head + 1]) * carried)
    kv = k_ref.shape[1]
    load.wait()
    for hop in list(range(1, members)) + [0]:
        place = lax.rem(mine + hop, members)
        piece = nn(y_b[...], w_ref[:, pl.ds(pl.multiple_of(place * kv, LANE), kv)])
        if hop:
            vp_send[hop] = rounded(piece)
            copy = remote(
                vp_send.at[hop], vp_recv.at[hop], p_s.at[hop], p_r.at[hop], group_id(place, sizes)
            )
            copy.start()
            sends.append(copy)
    for hop in range(1, members):
        place = lax.rem(mine + hop, members)
        remote(
            vp_send.at[hop], vp_recv.at[hop], p_s.at[hop], p_r.at[hop], group_id(place, sizes)
        ).wait_recv()
        piece = piece + vp_recv[hop].astype(F32)
    vall[me] = rounded(piece)
    for hop in range(1, ctx_count):
        peer = ctx_peer(me, hop, ctx_count)

        @pl.when(peer > me)
        def _():
            remote(vall.at[me], vall.at[me], v_s.at[hop], v_r.at[hop], {"ctx": peer}).start()

    for hop in range(1, ctx_count):
        source = ctx_peer(me, ctx_count - hop, ctx_count)

        @pl.when(source < me)
        def _():
            to = {"ctx": source}
            remote(kall.at[me], kall.at[source], k_s.at[hop], k_r.at[hop], to).wait_recv()
            remote(vall.at[me], vall.at[source], v_s.at[hop], v_r.at[hop], to).wait_recv()

    kall_out[...] = kall[...]
    vall_out[...] = vall[...]
    ent_out[...] = en_recv[...]
    decall_out[...] = decall[...]
    for copy in sends:
        copy.wait_send()
    for hop in range(1, ctx_count):
        peer = ctx_peer(me, hop, ctx_count)

        @pl.when(peer > me)
        def _():
            to = {"ctx": peer}
            remote(kall.at[me], kall.at[me], k_s.at[hop], k_r.at[hop], to).wait_send()
            remote(vall.at[me], vall.at[me], v_s.at[hop], v_r.at[hop], to).wait_send()


def attention_kernel(
    ctx_count, sizes,
    q_ref, do_ref, kall_ref, vall_ref,
    o_ref, dq_ref, dk_ref, vg_out,
    k_flip, v_flip, q_cat, do_cat, q_t, do_t, o_t, dq_t, s_buf, dk_acc, dv_acc, g_send, g_recv, vg_all,
    g_s, g_r, vg_s, vg_r,
):
    me = lax.axis_index("ctx")
    mine = group_place(sizes)
    members = sizes[0] * sizes[1]
    tok = q_ref.shape[0]
    seq = kall_ref.shape[0]
    kv_dev = kall_ref.shape[1] // LANE
    chunk = math.gcd(seq, 256)
    chunks = (me * tok + tok - 1) // chunk + 1
    scale_by = 1.0 / math.sqrt(LANE)
    cols = REP * tok
    g_recv[...] = jnp.zeros_like(g_recv)
    enter(ctx_count, sizes)
    query_pos = me * tok + lax.rem(lax.broadcasted_iota(jnp.int32, (chunk, cols), 1), tok)
    key_pos = lax.broadcasted_iota(jnp.int32, (chunk, cols), 0)

    for kv in range(kv_dev):
        span = slice(kv * LANE, (kv + 1) * LANE)
        spans = [slice((kv * REP + at) * LANE, (kv * REP + at + 1) * LANE) for at in range(REP)]
        for at, here in enumerate(spans):
            there = slice(at * tok, (at + 1) * tok)
            q_cat[there, :] = q_ref[:, here]
            do_cat[there, :] = do_ref[:, here]
            q_t[:, there] = flip(q_ref[:, here])
            do_t[:, there] = flip(do_ref[:, here])
        o_t[...] = jnp.zeros_like(o_t)
        dq_t[...] = jnp.zeros_like(dq_t)

        def scores(at, running):
            top, total = running
            here = pl.ds(pl.multiple_of(at * chunk, LANE), chunk)
            k_flip[:, here] = flip(kall_ref[here, span])
            v_flip[:, here] = flip(vall_ref[here, span])
            s = nn(kall_ref[here, span], q_t[...]) * scale_by
            s = jnp.where(key_pos + at * chunk <= query_pos, s, NEG_FILL)
            s_buf[here, :] = s
            new_top = jnp.maximum(top, jnp.max(s, axis=0, keepdims=True))
            block = jnp.sum(jnp.exp(s - new_top), axis=0, keepdims=True)
            return (new_top, total * jnp.exp(top - new_top) + block)

        top, total = lax.fori_loop(
            0, chunks, scores, (jnp.full((1, cols), NEG_FILL, F32), jnp.zeros((1, cols), F32))
        )
        inverse = 1.0 / total

        def outputs(at, carry):
            here = pl.ds(pl.multiple_of(at * chunk, LANE), chunk)
            p = jnp.exp(s_buf[here, :] - top) * inverse
            s_buf[here, :] = p
            p_b = rounded(p)
            dv_acc[here, span] = nn(p_b, do_cat[...])
            o_t[...] += nn(v_flip[:, here], p_b)
            return carry

        lax.fori_loop(0, chunks, outputs, 0)
        delta = jnp.sum(o_t[...] * do_t[...].astype(F32), axis=0, keepdims=True)

        def grads(at, carry):
            here = pl.ds(pl.multiple_of(at * chunk, LANE), chunk)
            dprobs = nn(vall_ref[here, span], do_t[...])
            ds = rounded(s_buf[here, :] * (dprobs - delta))
            dk_acc[here, span] = nn(ds, q_cat[...])
            dq_t[...] += nn(k_flip[:, here], ds)
            return carry

        lax.fori_loop(0, chunks, grads, 0)
        for hop in range(1, ctx_count):
            peer = ctx_peer(me, hop, ctx_count)

            @pl.when(peer < me)
            def _():
                block = pl.ds(pl.multiple_of(peer * tok, tok), tok)
                g_send[kv, hop, 0] = rounded(dk_acc[block, span])
                g_send[kv, hop, 1] = rounded(dv_acc[block, span])
                remote(
                    g_send.at[kv, hop], g_recv.at[kv, hop], g_s.at[kv, hop], g_r.at[kv, hop],
                    {"ctx": peer},
                ).start()

        for at, here in enumerate(spans):
            there = slice(at * tok, (at + 1) * tok)
            o_ref[:, here] = o_t[:, there].T
            dq_ref[:, here] = dq_t[:, there].T * scale_by
    own = pl.ds(pl.multiple_of(me * tok, tok), tok)
    for kv in range(kv_dev):
        span = slice(kv * LANE, (kv + 1) * LANE)
        dk = dk_acc[own, span]
        dv = dv_acc[own, span]
        for hop in range(1, ctx_count):
            source = ctx_peer(me, ctx_count - hop, ctx_count)

            @pl.when(source > me)
            def _():
                remote(
                    g_send.at[kv, hop], g_recv.at[kv, hop], g_s.at[kv, hop], g_r.at[kv, hop],
                    {"ctx": source},
                ).wait_recv()

            dk = dk + g_recv[kv, hop, 0].astype(F32)
            dv = dv + g_recv[kv, hop, 1].astype(F32)
        dk_ref[:, span] = dk * scale_by
        vg_all[mine, :, span] = rounded(dv)
    sends = []
    for hop in range(1, members):
        place = lax.rem(mine + hop, members)
        copy = remote(
            vg_all.at[mine], vg_all.at[mine], vg_s.at[hop], vg_r.at[hop], group_id(place, sizes)
        )
        copy.start()
        sends.append(copy)
    for hop in range(1, members):
        place = lax.rem(mine + members - hop, members)
        remote(
            vg_all.at[mine], vg_all.at[place], vg_s.at[hop], vg_r.at[hop], group_id(place, sizes)
        ).wait_recv()
    vg_out[...] = vg_all[...]
    for copy in sends:
        copy.wait_send()
    for kv in range(kv_dev):
        for hop in range(1, ctx_count):
            peer = ctx_peer(me, hop, ctx_count)

            @pl.when(peer < me)
            def _():
                remote(
                    g_send.at[kv, hop], g_recv.at[kv, hop], g_s.at[kv, hop], g_r.at[kv, hop],
                    {"ctx": peer},
                ).wait_send()


def backward_kernel(
    ctx_count,
    x_ref, b_ref, c_ref, cum_ref, cumt_ref, dt_ref, dtt_ref, skip_ref, w_hbm, ent_ref, decall, vg_ref,
    dx_ref, db_ref, dc_ref,
    g_acc, st_send, st_recv, en_send, en_recv,
    st_s, st_r, en_s, en_r, w_ref, w_s,
):
    me = lax.axis_index("ctx")
    tok = x_ref.shape[0]
    heads = x_ref.shape[1] // LANE
    groups = b_ref.shape[1] // LANE
    per_group = heads // groups
    rows = heads * LANE // ctx_count
    kv = vg_ref.shape[2]
    load = pltpu.make_async_copy(w_hbm, w_ref, w_s)
    load.start()
    enter_ctx(ctx_count)
    load.wait()
    for group in range(groups):
        wide = slice(group * per_group * LANE, (group + 1) * per_group * LANE)
        total = None
        for place in range(vg_ref.shape[0]):
            term = nt(vg_ref[place], w_ref[wide, place * kv:(place + 1) * kv])
            total = term if total is None else total + term
        g_acc[:, wide] = total
        c_flip = flip(c_ref[:, group * LANE:(group + 1) * LANE])
        for head in range(group * per_group, (group + 1) * per_group):
            span = slice(head * LANE, (head + 1) * LANE)
            scaled = rounded(jnp.exp(cum_ref[:, head:head + 1]) * g_acc[:, span])
            st_send[span, :] = rounded(nn(c_flip, scaled))
    sends = []
    for hop in range(1, ctx_count):
        peer = ctx_peer(me, hop, ctx_count)
        block = pl.ds(pl.multiple_of(peer * rows, 16), rows)
        copy = remote(st_send.at[block], st_recv.at[me], st_s.at[hop], st_r.at[hop], {"ctx": peer})
        copy.start()
        sends.append(copy)
    own_rows = pl.ds(pl.multiple_of(me * rows, 16), rows)
    st_recv[me] = st_send[own_rows, :]
    lower = triangle(tok, True)
    upper = triangle(tok, False)
    for group in range(groups):
        columns = slice(group * LANE, (group + 1) * LANE)
        b = b_ref[:, columns]
        c = c_ref[:, columns]
        inner_t = nt(b, c)
        inner_grad = jnp.zeros((tok, tok), F32)
        dc = jnp.zeros((tok, LANE), F32)
        for head in range(group * per_group, (group + 1) * per_group):
            span = slice(head * LANE, (head + 1) * LANE)
            cum = cum_ref[:, head:head + 1]
            cum_t = cumt_ref[head:head + 1, :]
            decays = jnp.where(lower, jnp.exp(jnp.where(lower, cum - cum_t, 0.0)), 0.0)
            decays_t = jnp.where(upper, jnp.exp(jnp.where(upper, cum_t - cum, 0.0)), 0.0)
            mixing_t = rounded(inner_t * decays_t * dt_ref[:, head:head + 1])
            g = g_acc[:, span]
            g_b = rounded(g)
            dx_ref[:, span] = nn(mixing_t, g_b) + skip_ref[:, head:head + 1] * g
            inner_grad = inner_grad + nt(g_b, x_ref[:, span]) * decays * dtt_ref[head:head + 1, :]
            dc = dc + nt(rounded(jnp.exp(cum) * g), ent_ref[span, :])
        dc_ref[:, columns] = dc + nn(rounded(inner_grad), b)
        db_ref[:, columns] = nn(rounded(inner_grad.T), c)
    for hop in range(1, ctx_count):
        peer = ctx_peer(me, ctx_count - hop, ctx_count)
        remote(
            st_send.at[pl.ds(0, rows)], st_recv.at[peer], st_s.at[hop], st_r.at[hop], {"ctx": peer}
        ).wait_recv()
    running = [jnp.zeros((part.stop - part.start, LANE), F32) for part, _ in scan_parts(me, rows)]
    for block in range(ctx_count - 1, -1, -1):
        for at, (part, head) in enumerate(scan_parts(me, rows)):
            en_send[block, part, :] = rounded(running[at])
            running[at] = (
                decall[block, pl.ds(head, 1), :] * running[at] + st_recv[block, part, :].astype(F32)
            )
    for hop in range(1, ctx_count):
        peer = ctx_peer(me, hop, ctx_count)
        copy = remote(
            en_send.at[peer], en_recv.at[own_rows], en_s.at[hop], en_r.at[hop], {"ctx": peer}
        )
        copy.start()
        sends.append(copy)
    en_recv[own_rows, :] = en_send[me]
    for hop in range(1, ctx_count):
        peer = ctx_peer(me, ctx_count - hop, ctx_count)
        block = pl.ds(pl.multiple_of(peer * rows, 16), rows)
        remote(
            en_send.at[0], en_recv.at[block], en_s.at[hop], en_r.at[hop], {"ctx": peer}
        ).wait_recv()
    for group in range(groups):
        columns = slice(group * LANE, (group + 1) * LANE)
        b = b_ref[:, columns]
        db = db_ref[:, columns]
        for head in range(group * per_group, (group + 1) * per_group):
            span = slice(head * LANE, (head + 1) * LANE)
            cum = cum_ref[:, head:head + 1]
            weight = jnp.exp(cum[tok - 1:tok, :] - cum) * dt_ref[:, head:head + 1]
            dstate = en_recv[span, :]
            dx_ref[:, span] += weight * nn(b, dstate)
            db = db + nt(rounded(x_ref[:, span].astype(F32) * weight), dstate)
        db_ref[:, columns] = db
    for copy in sends:
        copy.wait_send()


def body(
    sizes,
    mamba_x, mamba_b, mamba_c, step_dt, decay_a, skip_d, value_weight, queries, keys, out_grad
):
    tok = mamba_x.shape[0]
    heads = decay_a.shape[0]
    n = lax.axis_size("ctx")
    members = sizes[0] * sizes[1]
    kv = keys.shape[1]
    kv_dev = kv // LANE
    seq = n * tok
    rows = heads * LANE // n
    cum = jnp.cumsum(-step_dt * decay_a[None, :], axis=0)
    cum_t = cum.T
    dt_t = step_dt.T
    skip = skip_d[None, :]
    decay = jnp.broadcast_to(jnp.exp(cum[-1])[:, None], (heads, LANE))
    vmem = pl.BlockSpec(memory_space=pltpu.VMEM)
    dma = pltpu.SemaphoreType.DMA

    weight_slot = [pltpu.VMEM(value_weight.shape, BF16), dma]

    def call(kernel, operands, outs, scratch, ident):
        return pl.pallas_call(
            kernel,
            out_shape=[jax.ShapeDtypeStruct(shape, kind) for shape, kind in outs],
            in_specs=[
                pl.BlockSpec(memory_space=pl.ANY) if a is value_weight else vmem for a in operands
            ],
            out_specs=[vmem] * len(outs),
            scratch_shapes=scratch,
            compiler_params=pltpu.CompilerParams(
                collective_id=ident, has_side_effects=True, vmem_limit_bytes=VMEM_BYTES
            ),
        )(*operands)

    kall, vall, ent, decall = call(
        functools.partial(forward_kernel, n, sizes),
        (mamba_x, mamba_b, mamba_c, cum, cum_t, step_dt, dt_t, skip, decay, value_weight, keys),
        [((n, tok, kv), BF16), ((n, tok, kv), BF16), ((heads * LANE, LANE), BF16),
         ((n, heads, LANE), F32)],
        [
            pltpu.VMEM((n, tok, kv), BF16),
            pltpu.VMEM((n, tok, kv), BF16),
            pltpu.VMEM((n, heads, LANE), F32),
            pltpu.VMEM((heads * LANE, LANE), BF16),
            pltpu.VMEM((n, rows, LANE), BF16),
            pltpu.VMEM((n, rows, LANE), BF16),
            pltpu.VMEM((heads * LANE, LANE), BF16),
            pltpu.VMEM((tok, heads * LANE), F32),
            pltpu.VMEM((tok, heads * LANE), BF16),
            pltpu.VMEM((members, tok, kv), BF16),
            pltpu.VMEM((members, tok, kv), BF16),
        ] + [dma((n,))] * 10 + [dma((members,))] * 2 + weight_slot,
        0,
    )
    attn_out, grad_q, grad_k, vg = call(
        functools.partial(attention_kernel, n, sizes),
        (queries, out_grad, kall.reshape(seq, kv), vall.reshape(seq, kv)),
        [(queries.shape, F32), (queries.shape, F32), (keys.shape, F32), ((members, tok, kv), BF16)],
        [
            pltpu.VMEM((LANE, seq), BF16),
            pltpu.VMEM((LANE, seq), BF16),
            pltpu.VMEM((REP * tok, LANE), BF16),
            pltpu.VMEM((REP * tok, LANE), BF16),
            pltpu.VMEM((LANE, REP * tok), BF16),
            pltpu.VMEM((LANE, REP * tok), BF16),
            pltpu.VMEM((LANE, REP * tok), F32),
            pltpu.VMEM((LANE, REP * tok), F32),
            pltpu.VMEM((seq, REP * tok), F32),
            pltpu.VMEM((seq, kv), F32),
            pltpu.VMEM((seq, kv), F32),
            pltpu.VMEM((kv_dev, n, 2, tok, LANE), BF16),
            pltpu.VMEM((kv_dev, n, 2, tok, LANE), BF16),
            pltpu.VMEM((members, tok, kv), BF16),
            dma((kv_dev, n)), dma((kv_dev, n)), dma((members,)), dma((members,)),
        ],
        1,
    )
    grad_x, grad_b, grad_c = call(
        functools.partial(backward_kernel, n),
        (mamba_x, mamba_b, mamba_c, cum, cum_t, step_dt, dt_t, skip, value_weight, ent, decall, vg),
        [(mamba_x.shape, F32), (mamba_b.shape, F32), (mamba_c.shape, F32)],
        [
            pltpu.VMEM((tok, heads * LANE), F32),
            pltpu.VMEM((heads * LANE, LANE), BF16),
            pltpu.VMEM((n, rows, LANE), BF16),
            pltpu.VMEM((n, rows, LANE), BF16),
            pltpu.VMEM((heads * LANE, LANE), BF16),
        ] + [dma((n,))] * 4 + weight_slot,
        2,
    )
    return (attn_out, grad_q, grad_k, grad_x, grad_b, grad_c)


def solution(mesh):
    split = P("ctx", ("ch", "section"))
    per_head = P(("ch", "section"))
    in_specs = (
        split, split, split, split, per_head, per_head, P(("ch", "section"), None), split, split, split
    )
    sizes = (mesh.shape["ch"], mesh.shape["section"])
    return jax.shard_map(
        functools.partial(body, sizes),
        mesh=mesh, in_specs=in_specs, out_specs=(split,) * 6, check_vma=False,
    )
```

```python
import functools
import math

import jax
import jax.numpy as jnp
from jax import lax
from jax.experimental import pallas as pl
from jax.experimental.pallas import tpu as pltpu
from jax.sharding import PartitionSpec as P

LANE = 128
Q_HEADS = 64
KV_HEADS = 8
REP = Q_HEADS // KV_HEADS
NEG_FILL = -1e30
F32 = jnp.float32
BF16 = jnp.bfloat16
MESH = pl.DeviceIdType.MESH
VMEM_BYTES = 56 * 1024 * 1024


def nn(a, b):
    return lax.dot_general(a, b, (((1,), (0,)), ((), ())), preferred_element_type=F32)


def nt(a, b):
    return lax.dot_general(a, b, (((1,), (1,)), ((), ())), preferred_element_type=F32)


def flip(a):
    return a.astype(F32).T.astype(BF16)


def rounded(a):
    return a.astype(BF16)


def half_peer(me, hop, span):
    return me // span * span + lax.rem(me + hop, span)


def ctx_peer(me, hop, count):
    return lax.rem(me + hop, count)


def group_place(sizes):
    return lax.axis_index("ch") * sizes[1] + lax.axis_index("section")


def group_id(place, sizes):
    return {"ch": place // sizes[1], "section": lax.rem(place, sizes[1])}


def enter(ctx_count, sizes):
    me = lax.axis_index("ctx")
    mine = group_place(sizes)
    members = sizes[0] * sizes[1]
    barrier = pltpu.get_barrier_semaphore()
    for hop in range(1, ctx_count):
        pl.semaphore_signal(
            barrier, inc=1, device_id={"ctx": ctx_peer(me, hop, ctx_count)}, device_id_type=MESH
        )
    for hop in range(1, members):
        pl.semaphore_signal(
            barrier,
            inc=1,
            device_id=group_id(lax.rem(mine + hop, members), sizes),
            device_id_type=MESH,
        )
    pl.semaphore_wait(barrier, ctx_count + members - 2)


def enter_ctx(ctx_count):
    me = lax.axis_index("ctx")
    barrier = pltpu.get_barrier_semaphore()
    for hop in range(1, ctx_count):
        pl.semaphore_signal(
            barrier, inc=1, device_id={"ctx": ctx_peer(me, hop, ctx_count)}, device_id_type=MESH
        )
    pl.semaphore_wait(barrier, ctx_count - 1)


def remote(src, dst, send, recv, device):
    return pltpu.make_async_remote_copy(
        src_ref=src, dst_ref=dst, send_sem=send, recv_sem=recv, device_id=device, device_id_type=MESH
    )


def triangle(rows, lower):
    first = lax.broadcasted_iota(jnp.int32, (rows, rows), 0)
    second = lax.broadcasted_iota(jnp.int32, (rows, rows), 1)
    return first >= second if lower else second >= first


def scan_parts(me, rows):
    width = min(rows, LANE)
    for part in range(rows // width):
        yield slice(part * width, (part + 1) * width), (me * rows + part * width) // LANE


def forward_kernel(
    ctx_count, sizes,
    x_ref, b_ref, c_ref, cum_ref, cumt_ref, dt_ref, dtt_ref, skip_ref, dec_ref, w_hbm, k_ref,
    kall_out, vall_out, ent_out, decall_out,
    kall, vall, decall, st_send, st_recv, en_send, en_recv, y_acc, y_b, vp_send, vp_recv,
    st_s, st_r, en_s, en_r, k_s, k_r, v_s, v_r, d_s, d_r, p_s, p_r, w_ref, w_s, ca_send, ca_recv, ca_s, ca_r,
):
    me = lax.axis_index("ctx")
    mine = group_place(sizes)
    members = sizes[0] * sizes[1]
    tok = x_ref.shape[0]
    heads = x_ref.shape[1] // LANE
    per_group = heads // (b_ref.shape[1] // LANE)
    span_count = ctx_count // 2
    low = lax.rem(me, span_count)
    other = {"ctx": ctx_peer(me, span_count, ctx_count)}
    rows = heads * LANE // span_count
    ca_recv[...] = jnp.zeros_like(ca_recv)
    load = pltpu.make_async_copy(w_hbm, w_ref, w_s)
    load.start()
    kall[...] = jnp.zeros_like(kall)
    vall[...] = jnp.zeros_like(vall)
    decall[...] = jnp.zeros_like(decall)
    enter(ctx_count, sizes)
    decall[me] = dec_ref[...]
    kall[me] = k_ref[...]
    for head in range(heads):
        group = head // per_group
        if head % per_group == 0:
            b_flip = flip(b_ref[:, group * LANE:(group + 1) * LANE])
        cum = cum_ref[:, head:head + 1]
        weight = jnp.exp(cum[tok - 1:tok, :] - cum) * dt_ref[:, head:head + 1]
        xw = x_ref[:, head * LANE:(head + 1) * LANE].astype(F32) * weight
        st_send[head * LANE:(head + 1) * LANE, :] = rounded(nn(b_flip, rounded(xw)))
    sends = []
    for hop in range(1, span_count):
        peer = half_peer(me, hop, span_count)
        to = {"ctx": peer}
        copy = remote(decall.at[me], decall.at[me], d_s.at[hop], d_r.at[hop], to)
        copy.start()
        sends.append(copy)
        block = pl.ds(pl.multiple_of(lax.rem(peer, span_count) * rows, 16), rows)
        copy = remote(st_send.at[block], st_recv.at[low], st_s.at[hop], st_r.at[hop], to)
        copy.start()
        sends.append(copy)
    st_recv[low] = st_send[pl.ds(pl.multiple_of(low * rows, 16), rows), :]
    lower = triangle(tok, True)
    for head in range(heads):
        group = head // per_group
        if head % per_group == 0:
            columns = slice(group * LANE, (group + 1) * LANE)
            inner = nt(c_ref[:, columns], b_ref[:, columns])
        gap = cum_ref[:, head:head + 1] - cumt_ref[head:head + 1, :]
        decays = jnp.where(lower, jnp.exp(jnp.where(lower, gap, 0.0)), 0.0)
        mixing = inner * decays * dtt_ref[head:head + 1, :]
        high = rounded(mixing)
        rest = rounded(mixing - high.astype(F32))
        x_head = x_ref[:, head * LANE:(head + 1) * LANE]
        y_acc[:, head * LANE:(head + 1) * LANE] = (
            nn(high, x_head) + nn(rest, x_head) + skip_ref[:, head:head + 1] * x_head.astype(F32)
        )
    for hop in range(1, span_count):
        peer = half_peer(me, span_count - hop, span_count)
        to = {"ctx": peer}
        remote(decall.at[me], decall.at[peer], d_s.at[hop], d_r.at[hop], to).wait_recv()
        remote(
            st_send.at[pl.ds(0, rows)], st_recv.at[lax.rem(peer, span_count)], st_s.at[hop], st_r.at[hop], to
        ).wait_recv()
    @pl.when(me >= span_count)
    def _():
        remote(ca_send, ca_recv, ca_s, ca_r, other).wait_recv()

    running = [ca_recv[part, :].astype(F32) for part, _ in scan_parts(low, rows)]
    for block in range(span_count):
        for at, (part, head) in enumerate(scan_parts(low, rows)):
            en_send[block, part, :] = rounded(running[at])
            running[at] = (
                decall[me // span_count * span_count + block, pl.ds(head, 1), :] * running[at] + st_recv[block, part, :].astype(F32)
            )
    for at, (part, _) in enumerate(scan_parts(low, rows)):
        ca_send[part, :] = rounded(running[at])

    @pl.when(me < span_count)
    def _():
        remote(ca_send, ca_recv, ca_s, ca_r, other).start()

    own_rows = pl.ds(pl.multiple_of(low * rows, 16), rows)
    for hop in range(1, span_count):
        peer = half_peer(me, hop, span_count)
        copy = remote(
            en_send.at[lax.rem(peer, span_count)], en_recv.at[own_rows], en_s.at[hop], en_r.at[hop], {"ctx": peer}
        )
        copy.start()
        sends.append(copy)
    for hop in range(1, ctx_count):
        peer = ctx_peer(me, hop, ctx_count)

        @pl.when(peer > me)
        def _():
            remote(kall.at[me], kall.at[me], k_s.at[hop], k_r.at[hop], {"ctx": peer}).start()

    en_recv[own_rows, :] = en_send[low]
    for hop in range(1, span_count):
        peer = half_peer(me, span_count - hop, span_count)
        block = pl.ds(pl.multiple_of(lax.rem(peer, span_count) * rows, 16), rows)
        remote(
            en_send.at[0], en_recv.at[block], en_s.at[hop], en_r.at[hop], {"ctx": peer}
        ).wait_recv()
    for head in range(heads):
        group = head // per_group
        span = slice(head * LANE, (head + 1) * LANE)
        carried = nn(c_ref[:, group * LANE:(group + 1) * LANE], en_recv[span, :])
        y_b[:, span] = rounded(y_acc[:, span] + jnp.exp(cum_ref[:, head:head + 1]) * carried)
    kv = k_ref.shape[1]
    load.wait()
    for hop in list(range(1, members)) + [0]:
        place = lax.rem(mine + hop, members)
        piece = nn(y_b[...], w_ref[:, pl.ds(pl.multiple_of(place * kv, LANE), kv)])
        if hop:
            vp_send[hop] = rounded(piece)
            copy = remote(
                vp_send.at[hop], vp_recv.at[hop], p_s.at[hop], p_r.at[hop], group_id(place, sizes)
            )
            copy.start()
            sends.append(copy)
    for hop in range(1, members):
        place = lax.rem(mine + hop, members)
        remote(
            vp_send.at[hop], vp_recv.at[hop], p_s.at[hop], p_r.at[hop], group_id(place, sizes)
        ).wait_recv()
        piece = piece + vp_recv[hop].astype(F32)
    vall[me] = rounded(piece)
    for hop in range(1, ctx_count):
        peer = ctx_peer(me, hop, ctx_count)

        @pl.when(peer > me)
        def _():
            remote(vall.at[me], vall.at[me], v_s.at[hop], v_r.at[hop], {"ctx": peer}).start()

    for hop in range(1, ctx_count):
        source = ctx_peer(me, ctx_count - hop, ctx_count)

        @pl.when(source < me)
        def _():
            to = {"ctx": source}
            remote(kall.at[me], kall.at[source], k_s.at[hop], k_r.at[hop], to).wait_recv()
            remote(vall.at[me], vall.at[source], v_s.at[hop], v_r.at[hop], to).wait_recv()

    kall_out[...] = kall[...]
    vall_out[...] = vall[...]
    ent_out[...] = en_recv[...]
    decall_out[...] = decall[...]
    for copy in sends:
        copy.wait_send()

    @pl.when(me < span_count)
    def _():
        remote(ca_send, ca_recv, ca_s, ca_r, other).wait_send()

    for hop in range(1, ctx_count):
        peer = ctx_peer(me, hop, ctx_count)

        @pl.when(peer > me)
        def _():
            to = {"ctx": peer}
            remote(kall.at[me], kall.at[me], k_s.at[hop], k_r.at[hop], to).wait_send()
            remote(vall.at[me], vall.at[me], v_s.at[hop], v_r.at[hop], to).wait_send()


def attention_kernel(
    ctx_count, sizes,
    q_ref, do_ref, kall_ref, vall_ref,
    o_ref, dq_ref, dk_ref, vg_out,
    k_flip, v_flip, q_cat, do_cat, q_t, do_t, o_t, dq_t, s_buf, dk_acc, dv_acc, g_send, g_recv, vg_all,
    g_s, g_r, vg_s, vg_r,
):
    me = lax.axis_index("ctx")
    mine = group_place(sizes)
    members = sizes[0] * sizes[1]
    tok = q_ref.shape[0]
    seq = kall_ref.shape[0]
    kv_dev = kall_ref.shape[1] // LANE
    chunk = math.gcd(seq, 256)
    chunks = (me * tok + tok - 1) // chunk + 1
    scale_by = 1.0 / math.sqrt(LANE)
    cols = REP * tok
    g_recv[...] = jnp.zeros_like(g_recv)
    enter(ctx_count, sizes)
    query_pos = me * tok + lax.rem(lax.broadcasted_iota(jnp.int32, (chunk, cols), 1), tok)
    key_pos = lax.broadcasted_iota(jnp.int32, (chunk, cols), 0)

    for kv in range(kv_dev):
        span = slice(kv * LANE, (kv + 1) * LANE)
        spans = [slice((kv * REP + at) * LANE, (kv * REP + at + 1) * LANE) for at in range(REP)]
        for at, here in enumerate(spans):
            there = slice(at * tok, (at + 1) * tok)
            q_cat[there, :] = q_ref[:, here]
            do_cat[there, :] = do_ref[:, here]
            q_t[:, there] = flip(q_ref[:, here])
            do_t[:, there] = flip(do_ref[:, here])
        o_t[...] = jnp.zeros_like(o_t)
        dq_t[...] = jnp.zeros_like(dq_t)

        def scores(at, running):
            top, total = running
            here = pl.ds(pl.multiple_of(at * chunk, LANE), chunk)
            k_flip[:, here] = flip(kall_ref[here, span])
            v_flip[:, here] = flip(vall_ref[here, span])
            s = nn(kall_ref[here, span], q_t[...]) * scale_by
            s = jnp.where(key_pos + at * chunk <= query_pos, s, NEG_FILL)
            s_buf[here, :] = s
            new_top = jnp.maximum(top, jnp.max(s, axis=0, keepdims=True))
            block = jnp.sum(jnp.exp(s - new_top), axis=0, keepdims=True)
            return (new_top, total * jnp.exp(top - new_top) + block)

        top, total = lax.fori_loop(
            0, chunks, scores, (jnp.full((1, cols), NEG_FILL, F32), jnp.zeros((1, cols), F32))
        )
        inverse = 1.0 / total

        def outputs(at, carry):
            here = pl.ds(pl.multiple_of(at * chunk, LANE), chunk)
            p = jnp.exp(s_buf[here, :] - top) * inverse
            s_buf[here, :] = p
            p_b = rounded(p)
            dv_acc[here, span] = nn(p_b, do_cat[...])
            o_t[...] += nn(v_flip[:, here], p_b)
            return carry

        lax.fori_loop(0, chunks, outputs, 0)
        delta = jnp.sum(o_t[...] * do_t[...].astype(F32), axis=0, keepdims=True)

        def grads(at, carry):
            here = pl.ds(pl.multiple_of(at * chunk, LANE), chunk)
            dprobs = nn(vall_ref[here, span], do_t[...])
            ds = rounded(s_buf[here, :] * (dprobs - delta))
            dk_acc[here, span] = nn(ds, q_cat[...])
            dq_t[...] += nn(k_flip[:, here], ds)
            return carry

        lax.fori_loop(0, chunks, grads, 0)
        for hop in range(1, ctx_count):
            peer = ctx_peer(me, hop, ctx_count)

            @pl.when(peer < me)
            def _():
                block = pl.ds(pl.multiple_of(peer * tok, tok), tok)
                g_send[kv, hop, 0] = rounded(dk_acc[block, span])
                g_send[kv, hop, 1] = rounded(dv_acc[block, span])
                remote(
                    g_send.at[kv, hop], g_recv.at[kv, hop], g_s.at[kv, hop], g_r.at[kv, hop],
                    {"ctx": peer},
                ).start()

        for at, here in enumerate(spans):
            there = slice(at * tok, (at + 1) * tok)
            o_ref[:, here] = o_t[:, there].T
            dq_ref[:, here] = dq_t[:, there].T * scale_by
    own = pl.ds(pl.multiple_of(me * tok, tok), tok)
    for kv in range(kv_dev):
        span = slice(kv * LANE, (kv + 1) * LANE)
        dk = dk_acc[own, span]
        dv = dv_acc[own, span]
        for hop in range(1, ctx_count):
            source = ctx_peer(me, ctx_count - hop, ctx_count)

            @pl.when(source > me)
            def _():
                remote(
                    g_send.at[kv, hop], g_recv.at[kv, hop], g_s.at[kv, hop], g_r.at[kv, hop],
                    {"ctx": source},
                ).wait_recv()

            dk = dk + g_recv[kv, hop, 0].astype(F32)
            dv = dv + g_recv[kv, hop, 1].astype(F32)
        dk_ref[:, span] = dk * scale_by
        vg_all[mine, :, span] = rounded(dv)
    sends = []
    for hop in range(1, members):
        place = lax.rem(mine + hop, members)
        copy = remote(
            vg_all.at[mine], vg_all.at[mine], vg_s.at[hop], vg_r.at[hop], group_id(place, sizes)
        )
        copy.start()
        sends.append(copy)
    for hop in range(1, members):
        place = lax.rem(mine + members - hop, members)
        remote(
            vg_all.at[mine], vg_all.at[place], vg_s.at[hop], vg_r.at[hop], group_id(place, sizes)
        ).wait_recv()
    vg_out[...] = vg_all[...]
    for copy in sends:
        copy.wait_send()
    for kv in range(kv_dev):
        for hop in range(1, ctx_count):
            peer = ctx_peer(me, hop, ctx_count)

            @pl.when(peer < me)
            def _():
                remote(
                    g_send.at[kv, hop], g_recv.at[kv, hop], g_s.at[kv, hop], g_r.at[kv, hop],
                    {"ctx": peer},
                ).wait_send()


def backward_kernel(
    ctx_count,
    x_ref, b_ref, c_ref, cum_ref, cumt_ref, dt_ref, dtt_ref, skip_ref, w_hbm, ent_ref, decall, vg_ref,
    dx_ref, db_ref, dc_ref,
    g_acc, st_send, st_recv, en_send, en_recv,
    st_s, st_r, en_s, en_r, w_ref, w_s, ca_send, ca_recv, ca_s, ca_r,
):
    me = lax.axis_index("ctx")
    tok = x_ref.shape[0]
    heads = x_ref.shape[1] // LANE
    groups = b_ref.shape[1] // LANE
    per_group = heads // groups
    span_count = ctx_count // 2
    low = lax.rem(me, span_count)
    other = {"ctx": ctx_peer(me, span_count, ctx_count)}
    rows = heads * LANE // span_count
    ca_recv[...] = jnp.zeros_like(ca_recv)
    kv = vg_ref.shape[2]
    load = pltpu.make_async_copy(w_hbm, w_ref, w_s)
    load.start()
    enter_ctx(ctx_count)
    load.wait()
    for group in range(groups):
        wide = slice(group * per_group * LANE, (group + 1) * per_group * LANE)
        total = None
        for place in range(vg_ref.shape[0]):
            term = nt(vg_ref[place], w_ref[wide, place * kv:(place + 1) * kv])
            total = term if total is None else total + term
        g_acc[:, wide] = total
        c_flip = flip(c_ref[:, group * LANE:(group + 1) * LANE])
        for head in range(group * per_group, (group + 1) * per_group):
            span = slice(head * LANE, (head + 1) * LANE)
            scaled = rounded(jnp.exp(cum_ref[:, head:head + 1]) * g_acc[:, span])
            st_send[span, :] = rounded(nn(c_flip, scaled))
    sends = []
    for hop in range(1, span_count):
        peer = half_peer(me, hop, span_count)
        block = pl.ds(pl.multiple_of(lax.rem(peer, span_count) * rows, 16), rows)
        copy = remote(st_send.at[block], st_recv.at[low], st_s.at[hop], st_r.at[hop], {"ctx": peer})
        copy.start()
        sends.append(copy)
    own_rows = pl.ds(pl.multiple_of(low * rows, 16), rows)
    st_recv[low] = st_send[own_rows, :]
    lower = triangle(tok, True)
    upper = triangle(tok, False)
    for group in range(groups):
        columns = slice(group * LANE, (group + 1) * LANE)
        b = b_ref[:, columns]
        c = c_ref[:, columns]
        inner_t = nt(b, c)
        inner_grad = jnp.zeros((tok, tok), F32)
        dc = jnp.zeros((tok, LANE), F32)
        for head in range(group * per_group, (group + 1) * per_group):
            span = slice(head * LANE, (head + 1) * LANE)
            cum = cum_ref[:, head:head + 1]
            cum_t = cumt_ref[head:head + 1, :]
            decays = jnp.where(lower, jnp.exp(jnp.where(lower, cum - cum_t, 0.0)), 0.0)
            decays_t = jnp.where(upper, jnp.exp(jnp.where(upper, cum_t - cum, 0.0)), 0.0)
            mixing_t = rounded(inner_t * decays_t * dt_ref[:, head:head + 1])
            g = g_acc[:, span]
            g_b = rounded(g)
            dx_ref[:, span] = nn(mixing_t, g_b) + skip_ref[:, head:head + 1] * g
            inner_grad = inner_grad + nt(g_b, x_ref[:, span]) * decays * dtt_ref[head:head + 1, :]
            dc = dc + nt(rounded(jnp.exp(cum) * g), ent_ref[span, :])
        dc_ref[:, columns] = dc + nn(rounded(inner_grad), b)
        db_ref[:, columns] = nn(rounded(inner_grad.T), c)
    for hop in range(1, span_count):
        peer = half_peer(me, span_count - hop, span_count)
        remote(
            st_send.at[pl.ds(0, rows)], st_recv.at[lax.rem(peer, span_count)], st_s.at[hop], st_r.at[hop], {"ctx": peer}
        ).wait_recv()
    @pl.when(me < span_count)
    def _():
        remote(ca_send, ca_recv, ca_s, ca_r, other).wait_recv()

    running = [ca_recv[part, :].astype(F32) for part, _ in scan_parts(low, rows)]
    for block in range(span_count - 1, -1, -1):
        for at, (part, head) in enumerate(scan_parts(low, rows)):
            en_send[block, part, :] = rounded(running[at])
            running[at] = (
                decall[me // span_count * span_count + block, pl.ds(head, 1), :] * running[at] + st_recv[block, part, :].astype(F32)
            )
    for at, (part, _) in enumerate(scan_parts(low, rows)):
        ca_send[part, :] = rounded(running[at])

    @pl.when(me >= span_count)
    def _():
        remote(ca_send, ca_recv, ca_s, ca_r, other).start()

    for hop in range(1, span_count):
        peer = half_peer(me, hop, span_count)
        copy = remote(
            en_send.at[lax.rem(peer, span_count)], en_recv.at[own_rows], en_s.at[hop], en_r.at[hop], {"ctx": peer}
        )
        copy.start()
        sends.append(copy)
    en_recv[own_rows, :] = en_send[low]
    for hop in range(1, span_count):
        peer = half_peer(me, span_count - hop, span_count)
        block = pl.ds(pl.multiple_of(lax.rem(peer, span_count) * rows, 16), rows)
        remote(
            en_send.at[0], en_recv.at[block], en_s.at[hop], en_r.at[hop], {"ctx": peer}
        ).wait_recv()
    for group in range(groups):
        columns = slice(group * LANE, (group + 1) * LANE)
        b = b_ref[:, columns]
        db = db_ref[:, columns]
        for head in range(group * per_group, (group + 1) * per_group):
            span = slice(head * LANE, (head + 1) * LANE)
            cum = cum_ref[:, head:head + 1]
            weight = jnp.exp(cum[tok - 1:tok, :] - cum) * dt_ref[:, head:head + 1]
            dstate = en_recv[span, :]
            dx_ref[:, span] += weight * nn(b, dstate)
            db = db + nt(rounded(x_ref[:, span].astype(F32) * weight), dstate)
        db_ref[:, columns] = db
    for copy in sends:
        copy.wait_send()

    @pl.when(me >= span_count)
    def _():
        remote(ca_send, ca_recv, ca_s, ca_r, other).wait_send()


def body(
    sizes,
    mamba_x, mamba_b, mamba_c, step_dt, decay_a, skip_d, value_weight, queries, keys, out_grad
):
    tok = mamba_x.shape[0]
    heads = decay_a.shape[0]
    n = lax.axis_size("ctx")
    members = sizes[0] * sizes[1]
    kv = keys.shape[1]
    kv_dev = kv // LANE
    seq = n * tok
    half = n // 2
    rows = heads * LANE // half
    cum = jnp.cumsum(-step_dt * decay_a[None, :], axis=0)
    cum_t = cum.T
    dt_t = step_dt.T
    skip = skip_d[None, :]
    decay = jnp.broadcast_to(jnp.exp(cum[-1])[:, None], (heads, LANE))
    vmem = pl.BlockSpec(memory_space=pltpu.VMEM)
    dma = pltpu.SemaphoreType.DMA

    weight_slot = [
        pltpu.VMEM(value_weight.shape, BF16), dma,
        pltpu.VMEM((rows, LANE), BF16), pltpu.VMEM((rows, LANE), BF16), dma, dma,
    ]

    def call(kernel, operands, outs, scratch, ident):
        return pl.pallas_call(
            kernel,
            out_shape=[jax.ShapeDtypeStruct(shape, kind) for shape, kind in outs],
            in_specs=[
                pl.BlockSpec(memory_space=pl.ANY) if a is value_weight else vmem for a in operands
            ],
            out_specs=[vmem] * len(outs),
            scratch_shapes=scratch,
            compiler_params=pltpu.CompilerParams(
                collective_id=ident, has_side_effects=True, vmem_limit_bytes=VMEM_BYTES
            ),
        )(*operands)

    kall, vall, ent, decall = call(
        functools.partial(forward_kernel, n, sizes),
        (mamba_x, mamba_b, mamba_c, cum, cum_t, step_dt, dt_t, skip, decay, value_weight, keys),
        [((n, tok, kv), BF16), ((n, tok, kv), BF16), ((heads * LANE, LANE), BF16),
         ((n, heads, LANE), F32)],
        [
            pltpu.VMEM((n, tok, kv), BF16),
            pltpu.VMEM((n, tok, kv), BF16),
            pltpu.VMEM((n, heads, LANE), F32),
            pltpu.VMEM((heads * LANE, LANE), BF16),
            pltpu.VMEM((half, rows, LANE), BF16),
            pltpu.VMEM((half, rows, LANE), BF16),
            pltpu.VMEM((heads * LANE, LANE), BF16),
            pltpu.VMEM((tok, heads * LANE), F32),
            pltpu.VMEM((tok, heads * LANE), BF16),
            pltpu.VMEM((members, tok, kv), BF16),
            pltpu.VMEM((members, tok, kv), BF16),
        ] + [dma((n,))] * 10 + [dma((members,))] * 2 + weight_slot,
        0,
    )
    attn_out, grad_q, grad_k, vg = call(
        functools.partial(attention_kernel, n, sizes),
        (queries, out_grad, kall.reshape(seq, kv), vall.reshape(seq, kv)),
        [(queries.shape, F32), (queries.shape, F32), (keys.shape, F32), ((members, tok, kv), BF16)],
        [
            pltpu.VMEM((LANE, seq), BF16),
            pltpu.VMEM((LANE, seq), BF16),
            pltpu.VMEM((REP * tok, LANE), BF16),
            pltpu.VMEM((REP * tok, LANE), BF16),
            pltpu.VMEM((LANE, REP * tok), BF16),
            pltpu.VMEM((LANE, REP * tok), BF16),
            pltpu.VMEM((LANE, REP * tok), F32),
            pltpu.VMEM((LANE, REP * tok), F32),
            pltpu.VMEM((seq, REP * tok), F32),
            pltpu.VMEM((seq, kv), F32),
            pltpu.VMEM((seq, kv), F32),
            pltpu.VMEM((kv_dev, n, 2, tok, LANE), BF16),
            pltpu.VMEM((kv_dev, n, 2, tok, LANE), BF16),
            pltpu.VMEM((members, tok, kv), BF16),
            dma((kv_dev, n)), dma((kv_dev, n)), dma((members,)), dma((members,)),
        ],
        1,
    )
    grad_x, grad_b, grad_c = call(
        functools.partial(backward_kernel, n),
        (mamba_x, mamba_b, mamba_c, cum, cum_t, step_dt, dt_t, skip, value_weight, ent, decall, vg),
        [(mamba_x.shape, F32), (mamba_b.shape, F32), (mamba_c.shape, F32)],
        [
            pltpu.VMEM((tok, heads * LANE), F32),
            pltpu.VMEM((heads * LANE, LANE), BF16),
            pltpu.VMEM((half, rows, LANE), BF16),
            pltpu.VMEM((half, rows, LANE), BF16),
            pltpu.VMEM((heads * LANE, LANE), BF16),
        ] + [dma((n,))] * 4 + weight_slot,
        2,
    )
    return (attn_out, grad_q, grad_k, grad_x, grad_b, grad_c)


def solution(mesh):
    split = P("ctx", ("ch", "section"))
    per_head = P(("ch", "section"))
    in_specs = (
        split, split, split, split, per_head, per_head, P(("ch", "section"), None), split, split, split
    )
    sizes = (mesh.shape["ch"], mesh.shape["section"])
    return jax.shard_map(
        functools.partial(body, sizes),
        mesh=mesh, in_specs=in_specs, out_specs=(split,) * 6, check_vma=False,
    )
```
